768 devices in a mesh: rep: 16 (over x_lo, y), fsdp: 48 (over x_hi, z, core).
Axes of the slice: x: 4 (x_hi: 2, x_lo: 2; x = x_hi * 2 + x_lo), y: 8, z: 12, core: 2. Of those that a mesh axis runs over, the one named last changes fastest.
Arguments:
- tokens: bfloat16 [16, 12288, 8192], P('rep', 'fsdp'), may hold values from -6 to 6
- cotangent: bfloat16 [16, 12288, 288], P('rep', 'fsdp'), may hold values from -0.0546875 to 0.0546875
- weights: float32 [16, 2359296], P('rep', 'fsdp'), may hold values from -6 to 6
- start_weights: float32 [2359296], P('fsdp'), may hold values from -6 to 6
- momentum: float32 [2359296], P('fsdp'), may hold values from -6 to 6
Outputs:
- mixed_weights: float32 [16, 2359296], P('rep', 'fsdp')
- new_momentum: float32 [2359296], P('fsdp')
- new_start: float32 [2359296], P('fsdp')
The draws below stay inside these ranges and needn't reach their ends.
All inputs are finite; a program needn't handle non-finite values.
Results may differ from the reference program's by a relative error of at most 0.007.
Values may be sent and summed in bfloat16 or wider, within the bound.
A program may use at most 64 MiB of HBM per device.

```python
import jax
import jax.numpy as jnp
from jax import lax

D = 8192
HID = 288
FRAG = 2359296
TOKENS = 12288
N_REP = 16


def block_levels(key, dims, shards, least, high):
    level, own = 1.0, jax.random.fold_in(key, 6)
    for dim, blocks in shards:
        heights = jnp.exp(jax.random.uniform(jax.random.fold_in(own, dim), (blocks,), jnp.float32, least / len(shards), high / len(shards)))
        level = level * jnp.repeat(heights, dims[dim] // blocks).reshape([-1 if axis == dim else 1 for axis in range(len(dims))])
    return level


def normal_values(rng, shape, width, most, cuts=(), held_as=jnp.bfloat16):
    values = jax.random.normal(rng, shape, jnp.float32) * width
    if len(cuts) > 0:
        values = block_levels(rng, shape, cuts, -0.22, 0.18) * values
    return jnp.clip(values, min=-most, max=most).astype(held_as)


def setup_inputs(seed: int = 0) -> dict:
    splits = jax.random.split(jax.random.key(seed), 6)
    return {
        "tokens": normal_values(splits[0], (N_REP, TOKENS, D), 1.0, 6.0, ((0, 16), (1, 48))),
        "cotangent": normal_values(splits[1], (N_REP, TOKENS, HID), TOKENS ** -0.5, 0.0546875, ((0, 16), (1, 48))),
        "weights": normal_values(splits[2], (N_REP, FRAG), 1.0, 6.0, ((0, 16), (1, 48)), jnp.float32),
        "start_weights": normal_values(splits[3], (FRAG,), 1.0, 6.0, ((0, 48),), jnp.float32),
        "momentum": normal_values(splits[4], (FRAG,), 1.0, 6.0, ((0, 48),), jnp.float32),
    }


code_limit = 448.0
scale_eps = 1e-6
inner_rate = 0.5
outer_rate = 0.7
nesterov_mu = 0.9
mix_weight = 0.5


def decode_delta(start_weights, replica_weights):
    delta_rows = (start_weights - replica_weights).reshape(-1, 128)
    block_scale = (jnp.max(jnp.abs(delta_rows), axis=1) / code_limit + scale_eps).astype(jnp.bfloat16)
    scale_wide = block_scale.astype(jnp.float32)[:, None]
    code_rows = (delta_rows / scale_wide).astype(jnp.bfloat16)
    return (code_rows.astype(jnp.float32) * scale_wide).reshape(-1)


def reference(tokens, cotangent, weights, start_weights, momentum):
    def add_replica(carry, replica_weights):
        return carry + decode_delta(start_weights, replica_weights), None

    summed, _ = lax.scan(add_replica, jnp.zeros(start_weights.shape, jnp.float32), weights)
    average = summed / N_REP
    new_momentum = nesterov_mu * momentum + average
    new_start = start_weights - outer_rate * (nesterov_mu * new_momentum + average)

    def inner_step(items):
        tok_rows, cot_rows, replica_weights = items
        grad = lax.dot_general(tok_rows, cot_rows, (((0,), (0,)), ((), ())), preferred_element_type=jnp.float32)
        current = replica_weights - inner_rate * grad.reshape(-1)
        return mix_weight * current + (1.0 - mix_weight) * new_start

    mixed_weights = lax.map(inner_step, (tokens, cotangent, weights))
    return mixed_weights, new_momentum, new_start
```

```python
import jax
import jax.numpy as jnp
from jax import lax
from jax.experimental import pallas as pl
from jax.experimental.pallas import tpu as pltpu
from jax.sharding import PartitionSpec as P

code_limit = 448.0
scale_eps = 1e-06
inner_rate = 0.5
outer_rate = 0.7
nesterov_mu = 0.9
mix_weight = 0.5

MESH = pl.DeviceIdType.MESH
NZ = 12
LANES = 128
SHARD = 384
LATE = 192
EARLY = SHARD - LATE
STEPS = (-2, -1, 1, 2)
SPAN = 512
SPANS = 8
HOPS = NZ // 2


def flatten_span(S, flat, lanes):
    A = [[S[j, pl.ds(k, 128, stride=4), :] for j in range(3)] for k in range(4)]
    R = [A[0]] + [[pltpu.roll(A[k][j], 32 * k, 1) for j in range(3)] for k in (1, 2, 3)]
    m32, m64, m96 = lanes < 32, lanes < 64, lanes < 96
    tiles = [
        R[0][0],
        R[0][1],
        jnp.where(m32, R[0][2], R[1][0]),
        jnp.where(m32, R[1][0], R[1][1]),
        jnp.where(m32, R[1][1], jnp.where(m64, R[1][2], R[2][0])),
        jnp.where(m64, R[2][0], R[2][1]),
        jnp.where(m64, R[2][1], jnp.where(m96, R[2][2], R[3][0])),
        jnp.where(m96, R[3][0], R[3][1]),
        jnp.where(m96, R[3][1], R[3][2]),
    ]
    for j in range(9):
        flat[pl.ds(j, 128, stride=9), :] = tiles[j]


def kernel(
    tok_hbm, cot_hbm, w_hbm, s_hbm,
    grad_hbm, avg_hbm,
    tok2, cot2, cot, wv, sv, dec, avg, ry, rx, S, flat, A, B, XB, ring_a, ring_b, Fa, Fb, xa, xb, grad,
    local_sem, tok_send, tok_recv, cot_send, cot_recv, y_send, y_recv, x_send, x_recv,
    near_sem, g_send, g_recv, b_send, b_recv, ra_send, ra_recv, rb_send, rb_recv, fin_send, fin_recv,
):
    f32 = jnp.float32
    NY = ry.shape[0] + 1
    PIECE = SHARD // NY
    rounds = NY // 2 - 1
    rep = lax.axis_index("rep")
    pos = lax.axis_index("fsdp")
    xl, y = rep // NY, rep % NY
    a, z, c = pos // (2 * NZ), (pos % (2 * NZ)) // 2, pos % 2
    own = c == a
    other = jnp.logical_not(own)

    partner = (rep, pos + 1 - 2 * c)
    z_next = (rep, a * 2 * NZ + ((z + 1) % NZ) * 2 + c)
    z_prev = (rep, a * 2 * NZ + ((z + NZ - 1) % NZ) * 2 + c)
    x_near = ((1 - xl) * NY + y, pos)

    def x_far(core):
        return (rep, (1 - a) * 2 * NZ + z * 2 + core)

    def y_peer(d):
        return (xl * NY + (y + d) % NY, pos)

    def remote(src, dst, send, recv, device):
        return pltpu.make_async_remote_copy(
            src_ref=src, dst_ref=dst, send_sem=send, recv_sem=recv, device_id=device, device_id_type=MESH
        )

    w_copy = pltpu.make_async_copy(w_hbm, wv, local_sem.at[0])
    s_copy = pltpu.make_async_copy(s_hbm, sv, local_sem.at[1])
    cot_copy = pltpu.make_async_copy(cot_hbm, cot2.at[:, pl.ds(0, 256)], local_sem.at[2])
    half = SPAN * SPANS
    tok_copy = pltpu.make_async_copy(
        tok_hbm.at[:, pl.ds(pl.multiple_of(c * half, half), half)], tok2.at[pl.ds(0, 256)], local_sem.at[3]
    )
    cot_copy.start()
    tok_copy.start()
    w_copy.start()
    s_copy.start()

    turn = NY // 2
    place = jnp.where(y < turn, y, NY + turn - 1 - y)

    def y_near(o):
        at = place + o
        return (xl * NY + jnp.where(at < turn, at, NY + turn - 1 - at), pos)

    def each_near(act):
        for j, o in enumerate(STEPS):

            @pl.when((place + o >= 0) & (place + o < NY))
            def _():
                act(j, o)

    barrier = pltpu.get_barrier_semaphore()
    for dev in (partner, z_next, z_prev, x_near, x_far(0), x_far(1)):
        pl.semaphore_signal(barrier, inc=1, device_id=dev, device_id_type=MESH)
    each_near(lambda j, o: pl.semaphore_signal(barrier, inc=1, device_id=y_near(o), device_id_type=MESH))
    n_near = jnp.minimum(place, 2) + jnp.minimum(NY - 1 - place, 2)

    def pass_on(r):
        if r < rounds:
            each_near(
                lambda j, o: pl.semaphore_signal(
                    near_sem.at[3 - j, r], inc=1, device_id=y_near(o), device_id_type=MESH
                )
            )

    def heard(r):
        if r < rounds:
            each_near(lambda j, o: pl.semaphore_wait(near_sem.at[j, r], 1))

    far = (z + HOPS) % NZ

    def pick(table, i):
        return sum(jnp.where(i == j, v, 0) for j, v in enumerate(table))

    def span_at(i):
        outer = pick((0, 1, -1, -2, 2, -3, 3, 4), i)
        inner = pick((0, 1, 2, -1, 3, -2, 4, -3), i)
        third = far % 3
        o = jnp.where(third == 1, inner, jnp.where(third == 0, outer, 1 - outer))
        return (2 * (far // 3) + o + 2 * SPANS) % SPANS

    def tok_remote(i):
        t = span_at(i)
        return remote(
            tok_hbm.at[:, pl.ds(pl.multiple_of((1 - c) * half + t * SPAN, SPAN), SPAN)],
            tok2.at[pl.ds(256, 256), pl.ds(pl.multiple_of(t * SPAN, SPAN), SPAN)],
            tok_send.at[i],
            tok_recv.at[i],
            partner,
        )

    cot_remote = remote(cot_hbm, cot2.at[:, pl.ds(256, 256)], cot_send, cot_recv, partner)

    def y_remote(d):
        return remote(
            dec.at[pl.ds(pl.multiple_of(((y + d) % NY) * PIECE, 8), PIECE)],
            ry.at[d - 1],
            y_send.at[d - 1],
            y_recv.at[d - 1],
            y_peer(d),
        )

    mine = pl.ds(pl.multiple_of(y * PIECE, 8), PIECE)
    x_remote = remote(rx.at[0], rx.at[1], x_send, x_recv, x_near)

    def g_remote(d):
        return remote(avg.at[mine], avg.at[mine], g_send.at[d - 1], g_recv.at[d - 1], y_peer(d))

    def b_remote(i):
        rows = pl.ds(3 * span_at(i), 3)
        return remote(B.at[rows], XB.at[rows], b_send.at[i], b_recv.at[i], x_far(c))

    def dest_at(way, s):
        return (z + HOPS - s) % NZ if way == 0 else (z + NZ - HOPS + s) % NZ

    def ring_remote(P_, way, k, s):
        buf, ring, send, recv = P_
        return remote(
            buf.at[dest_at(way, s) * 2 + k],
            ring.at[way, k, s],
            send.at[way, k, s],
            recv.at[way, k, s],
            z_next if way == 0 else z_prev,
        )

    part_a = (A, ring_a, ra_send, ra_recv)
    part_b = (B, ring_b, rb_send, rb_recv)
    order = ((0, 0), (1, 1), (1, 0), (0, 1))

    def ring_step(P_, way, k, s):
        buf, ring = P_[:2]
        ring_remote(P_, way, k, s - 1).wait_recv()
        at = dest_at(way, s) * 2 + k
        buf[at] = (buf[at].astype(f32) + ring[way, k, s - 1].astype(f32)).astype(buf.dtype)
        ring_remote(P_, way, k, s).start()
        ring_remote(P_, way, k, s - 1).wait_send()

    def ring_0(P_):
        ring_remote(P_, 0, 0, 0).start()
        ring_remote(P_, 1, 1, 0).start()

    def ring_1(P_):
        ring_remote(P_, 0, 1, 1).start()
        ring_remote(P_, 1, 0, 1).start()
        ring_step(P_, 0, 0, 1)
        ring_step(P_, 1, 1, 1)

    def ring_s(P_, s):
        for way, k in order:
            ring_step(P_, way, k, s)

    lanes = lax.broadcasted_iota(jnp.int32, (128, LANES), 1)

    def do_spans(lo, hi):
        @pl.loop(lo, hi)
        def _(i):
            t = span_at(i)
            tok_remote(i).wait_recv()
            for q in range(4):
                X = tok2[:, pl.ds(pl.multiple_of(t * SPAN + 128 * q, 128), 128)]
                out = lax.dot_general(X, cot[...], (((0,), (0,)), ((), ())), preferred_element_type=f32)
                for j in range(2):
                    S[j, 128 * q : 128 * q + 128, :] = out[:, 128 * j : 128 * j + 128]
                S[2, 128 * q : 128 * q + 128, 0:32] = out[:, 256:288]
            flatten_span(S, flat, lanes)
            for j in range(3):
                A[3 * t + j] = flat[SHARD * j : SHARD * j + LATE, :].astype(A.dtype)
                B[3 * t + j] = flat[SHARD * j + LATE : SHARD * (j + 1), :].astype(B.dtype)

            @pl.when(other)
            def _():
                b_remote(i).start()

    def add_spans(lo, hi):
        @pl.loop(lo, hi)
        def _(i):
            t = span_at(i)
            b_remote(i).wait_recv()
            for j in range(3):
                B[3 * t + j] = (B[3 * t + j].astype(f32) + XB[3 * t + j].astype(f32)).astype(B.dtype)

    pl.semaphore_wait(barrier, 6 + n_near)
    cot_remote.start()

    @pl.loop(0, SPANS)
    def _(i):
        tok_remote(i).start()

    pass_on(0)
    S[2] = jnp.zeros((SPAN, LANES), f32)
    tok_copy.wait()
    cot_copy.wait()
    cot_remote.wait_recv()
    cot[...] = cot2[...].astype(f32).T.astype(cot.dtype)

    do_spans(0, 2)
    ring_0(part_a)
    heard(0)
    pass_on(1)

    w_copy.wait()
    s_copy.wait()
    delta = sv[...] - wv[...]
    scale = (jnp.max(jnp.abs(delta), axis=1, keepdims=True) / code_limit + scale_eps).astype(jnp.bfloat16)
    scale = scale.astype(f32)
    dec[...] = (delta / scale).astype(jnp.bfloat16).astype(f32) * scale

    do_spans(2, 3)
    ring_1(part_a)
    do_spans(3, 6)
    heard(1)
    pass_on(2)

    @pl.when(own)
    def _():
        add_spans(0, 2)
        ring_0(part_b)

    ring_s(part_a, 2)
    do_spans(6, 8)

    @pl.when(own)
    def _():
        add_spans(2, 3)
        ring_1(part_b)

    ring_s(part_a, 3)
    heard(2)

    @pl.loop(1, NY)
    def _(d):
        y_remote(d).start()

    @pl.when(own)
    def _():
        add_spans(3, 4)
        ring_s(part_b, 2)

    ring_s(part_a, 4)

    @pl.loop(0, SPANS)
    def _(i):
        tok_remote(i).wait_send()

    cot_remote.wait_send()

    @pl.when(own)
    def _():
        add_spans(4, 6)
        ring_s(part_b, 3)

    ring_s(part_a, 5)

    @pl.loop(1, NY)
    def _(d):
        y_remote(d).wait()

    total = dec[mine, :]
    for d in range(NY - 1):
        total = total + ry[d]
    rx[0] = total
    x_remote.start()

    @pl.when(own)
    def _():
        add_spans(6, 7)
        ring_s(part_b, 4)

    def spread():
        x_remote.wait()
        avg[mine, :] = (rx[0] + rx[1]) / (2 * NY)

        @pl.loop(1, NY)
        def _(d):
            g_remote(d).start()

    @pl.when(own)
    def _():
        spread()
        add_spans(7, 8)
        ring_s(part_b, 5)

    def fin(P_, k, slot, dst, device):
        return remote((Fa if P_ is part_a else Fb).at[k], dst, fin_send.at[slot], fin_recv.at[slot], device)

    def a_partner(k):
        return fin(part_a, k, 0, xa.at[0], partner)

    def a_far(k):
        return remote(Fa.at[k], xa.at[1], fin_send.at[1 + k], fin_recv.at[1], x_far(k))

    def b_partner(k):
        return fin(part_b, k, 3, xb, partner)

    def finish(P_, k):
        buf, ring = P_[:2]
        ring_remote(P_, 0, k, HOPS - 1).wait_recv()
        ring_remote(P_, 1, k, HOPS - 1).wait_recv()
        return buf[z * 2 + k].astype(f32) + ring[0, k, HOPS - 1].astype(f32) + ring[1, k, HOPS - 1].astype(f32)

    near_first = jnp.where(own, 1 - c, 0)
    for k in (near_first, 1 - near_first):
        Fa[k] = finish(part_a, k).astype(Fa.dtype)

        @pl.when(other)
        def _():
            a_far(k).start()

        @pl.when(own & (c != k))
        def _():
            a_partner(k).start()

    @pl.when(other)
    def _():
        spread()

    @pl.when(own)
    def _():
        Fb[1 - c] = finish(part_b, 1 - c).astype(Fb.dtype)
        b_partner(1 - c).start()
        grad[LATE:, :] = finish(part_b, c)

    a_far(0).wait_recv()

    @pl.when(own)
    def _():
        grad[:LATE, :] = Fa[c].astype(f32) + xa[1].astype(f32)

    @pl.when(other)
    def _():
        a_partner(0).wait_recv()
        grad[:LATE, :] = xa[0].astype(f32) + xa[1].astype(f32)
        b_partner(0).wait_recv()
        grad[LATE:, :] = xb[...].astype(f32)

    grad_copy = pltpu.make_async_copy(grad, grad_hbm, local_sem.at[5])
    grad_copy.start()

    @pl.loop(1, NY)
    def _(d):
        g_remote(d).wait()

    avg_copy = pltpu.make_async_copy(avg, avg_hbm, local_sem.at[4])
    avg_copy.start()

    def ring_sent(P_):
        for way, k in order:
            ring_remote(P_, way, k, HOPS - 1).wait_send()

    ring_sent(part_a)

    @pl.when(own)
    def _():
        a_partner(0).wait_send()
        b_partner(0).wait_send()
        ring_sent(part_b)

    @pl.when(other)
    def _():
        a_far(0).wait_send()
        a_far(1).wait_send()

        @pl.loop(0, SPANS)
        def _(i):
            b_remote(i).wait_send()

    avg_copy.wait()
    grad_copy.wait()


def body(tokens, cotangent, weights, start_weights, momentum):
    shape = (SHARD, LANES)
    ny = lax.axis_size("rep") // 2
    piece = SHARD // ny
    f32, bf16 = jnp.float32, jnp.bfloat16
    dma = pltpu.SemaphoreType.DMA
    out = jax.ShapeDtypeStruct(shape, f32)
    late, early = (LATE, LANES), (EARLY, LANES)
    shards = 2 * NZ
    grad, average = pl.pallas_call(
        kernel,
        out_shape=(out, out),
        in_specs=[pl.BlockSpec(memory_space=pltpu.HBM)] * 4,
        out_specs=[pl.BlockSpec(memory_space=pltpu.HBM)] * 2,
        scratch_shapes=[
            pltpu.VMEM((512, SPAN * SPANS), bf16),
            pltpu.VMEM((288, 512), bf16),
            pltpu.VMEM((512, 288), bf16),
            pltpu.VMEM(shape, f32),
            pltpu.VMEM(shape, f32),
            pltpu.VMEM(shape, f32),
            pltpu.VMEM(shape, f32),
            pltpu.VMEM((ny - 1, piece, LANES), f32),
            pltpu.VMEM((2, piece, LANES), f32),
            pltpu.VMEM((3, SPAN, LANES), f32),
            pltpu.VMEM((1152, LANES), f32),
            pltpu.VMEM((shards, *late), bf16),
            pltpu.VMEM((shards, *early), bf16),
            pltpu.VMEM((shards, *early), bf16),
            pltpu.VMEM((2, 2, HOPS, *late), bf16),
            pltpu.VMEM((2, 2, HOPS, *early), bf16),
            pltpu.VMEM((2, *late), bf16),
            pltpu.VMEM((2, *early), bf16),
            pltpu.VMEM((2, *late), bf16),
            pltpu.VMEM(early, bf16),
            pltpu.VMEM(shape, f32),
            dma((6,)),
            dma((SPANS,)),
            dma((SPANS,)),
            dma,
            dma,
            dma((ny - 1,)),
            dma((ny - 1,)),
            dma,
            dma,
            pltpu.SemaphoreType.REGULAR((len(STEPS), max(ny // 2 - 1, 1))),
            dma((ny - 1,)),
            dma((ny - 1,)),
            dma((SPANS,)),
            dma((SPANS,)),
            dma((2, 2, HOPS)),
            dma((2, 2, HOPS)),
            dma((2, 2, HOPS)),
            dma((2, 2, HOPS)),
            dma((4,)),
            dma((4,)),
        ],
        compiler_params=pltpu.CompilerParams(
            collective_id=0, has_side_effects=True, vmem_limit_bytes=60 << 20
        ),
    )(tokens[0], cotangent[0].T, weights.reshape(shape), start_weights.reshape(shape))
    grad, average = grad.reshape(-1), average.reshape(-1)
    new_momentum = nesterov_mu * momentum + average
    new_start = start_weights - outer_rate * (nesterov_mu * new_momentum + average)
    current = weights[0] - inner_rate * grad
    mixed_weights = mix_weight * current + (1.0 - mix_weight) * new_start
    return mixed_weights[None], new_momentum, new_start


def solution(mesh):
    placed = (
        P("rep", "fsdp", None),
        P("rep", "fsdp", None),
        P("rep", "fsdp"),
        P("fsdp"),
        P("fsdp"),
    )
    return jax.shard_map(
        body,
        mesh=mesh,
        in_specs=placed,
        out_specs=(P("rep", "fsdp"), P("fsdp"), P("fsdp")),
        check_vma=False,
    )
```

```python
import jax
import jax.numpy as jnp
from jax import lax
from jax.experimental import pallas as pl
from jax.experimental.pallas import tpu as pltpu
from jax.sharding import PartitionSpec as P

code_limit = 448.0
scale_eps = 1e-06
inner_rate = 0.5
outer_rate = 0.7
nesterov_mu = 0.9
mix_weight = 0.5

MESH = pl.DeviceIdType.MESH
NZ = 12
LANES = 128
SHARD = 384
LATE = 192
EARLY = SHARD - LATE
STEPS = (-2, -1, 1, 2)
SPAN = 512
SPANS = 8
HOPS = NZ // 2


def flatten_span(S, flat, lanes):
    A = [[S[j, pl.ds(k, 128, stride=4), :] for j in range(3)] for k in range(4)]
    R = [A[0]] + [[pltpu.roll(A[k][j], 32 * k, 1) for j in range(3)] for k in (1, 2, 3)]
    m32, m64, m96 = lanes < 32, lanes < 64, lanes < 96
    tiles = [
        R[0][0],
        R[0][1],
        jnp.where(m32, R[0][2], R[1][0]),
        jnp.where(m32, R[1][0], R[1][1]),
        jnp.where(m32, R[1][1], jnp.where(m64, R[1][2], R[2][0])),
        jnp.where(m64, R[2][0], R[2][1]),
        jnp.where(m64, R[2][1], jnp.where(m96, R[2][2], R[3][0])),
        jnp.where(m96, R[3][0], R[3][1]),
        jnp.where(m96, R[3][1], R[3][2]),
    ]
    for j in range(9):
        flat[pl.ds(j, 128, stride=9), :] = tiles[j]


def kernel(
    tok_hbm, cot_hbm, w_hbm, s_hbm,
    grad_hbm, avg_hbm,
    tok2, cot2, cot, wv, sv, dec, avg, ry, rx, S, flat, A, B, XB, ring_a, ring_b, Fa, Fb, xa, xb, grad,
    local_sem, tok_send, tok_recv, cot_send, cot_recv, y_send, y_recv, x_send, x_recv,
    near_sem, g_send, g_recv, b_send, b_recv, ra_send, ra_recv, rb_send, rb_recv, fin_send, fin_recv,
):
    f32 = jnp.float32
    NY = ry.shape[0] + 1
    PIECE = SHARD // NY
    rounds = NY // 2 - 1
    rep = lax.axis_index("rep")
    pos = lax.axis_index("fsdp")
    xl, y = rep // NY, rep % NY
    a, z, c = pos // (2 * NZ), (pos % (2 * NZ)) // 2, pos % 2
    own = c == a
    other = jnp.logical_not(own)

    partner = (rep, pos + 1 - 2 * c)
    z_next = (rep, a * 2 * NZ + ((z + 1) % NZ) * 2 + c)
    z_prev = (rep, a * 2 * NZ + ((z + NZ - 1) % NZ) * 2 + c)
    x_near = ((1 - xl) * NY + y, pos)

    def x_far(core):
        return (rep, (1 - a) * 2 * NZ + z * 2 + core)

    def y_peer(d):
        return (xl * NY + (y + d) % NY, pos)

    def remote(src, dst, send, recv, device):
        return pltpu.make_async_remote_copy(
            src_ref=src, dst_ref=dst, send_sem=send, recv_sem=recv, device_id=device, device_id_type=MESH
        )

    w_copy = pltpu.make_async_copy(w_hbm, wv, local_sem.at[0])
    s_copy = pltpu.make_async_copy(s_hbm, sv, local_sem.at[1])
    cot_copy = pltpu.make_async_copy(cot_hbm, cot2.at[:, pl.ds(0, 256)], local_sem.at[2])
    half = SPAN * SPANS
    tok_copy = pltpu.make_async_copy(
        tok_hbm.at[:, pl.ds(pl.multiple_of(c * half, half), half)], tok2.at[pl.ds(0, 256)], local_sem.at[3]
    )
    cot_copy.start()
    tok_copy.start()
    w_copy.start()
    s_copy.start()

    turn = NY // 2
    place = jnp.where(y < turn, y, NY + turn - 1 - y)

    def y_near(o):
        at = place + o
        return (xl * NY + jnp.where(at < turn, at, NY + turn - 1 - at), pos)

    def each_near(act):
        for j, o in enumerate(STEPS):

            @pl.when((place + o >= 0) & (place + o < NY))
            def _():
                act(j, o)

    barrier = pltpu.get_barrier_semaphore()
    for dev in (partner, z_next, z_prev, x_near, x_far(0), x_far(1)):
        pl.semaphore_signal(barrier, inc=1, device_id=dev, device_id_type=MESH)
    each_near(lambda j, o: pl.semaphore_signal(barrier, inc=1, device_id=y_near(o), device_id_type=MESH))
    n_near = jnp.minimum(place, 2) + jnp.minimum(NY - 1 - place, 2)

    def pass_on(r):
        if r < rounds:
            each_near(
                lambda j, o: pl.semaphore_signal(
                    near_sem.at[3 - j, r], inc=1, device_id=y_near(o), device_id_type=MESH
                )
            )

    def heard(r):
        if r < rounds:
            each_near(lambda j, o: pl.semaphore_wait(near_sem.at[j, r], 1))

    far = (z + HOPS) % NZ

    def pick(table, i):
        return sum(jnp.where(i == j, v, 0) for j, v in enumerate(table))

    def span_at(i):
        outer = pick((0, 1, -1, -2, 2, -3, 3, 4), i)
        inner = pick((0, 1, 2, -1, 3, -2, 4, -3), i)
        third = far % 3
        o = jnp.where(third == 1, inner, jnp.where(third == 0, outer, 1 - outer))
        return (2 * (far // 3) + o + 2 * SPANS) % SPANS

    def tok_remote(i):
        t = span_at(i)
        return remote(
            tok_hbm.at[:, pl.ds(pl.multiple_of((1 - c) * half + t * SPAN, SPAN), SPAN)],
            tok2.at[pl.ds(256, 256), pl.ds(pl.multiple_of(t * SPAN, SPAN), SPAN)],
            tok_send.at[i],
            tok_recv.at[i],
            partner,
        )

    cot_remote = remote(cot_hbm, cot2.at[:, pl.ds(256, 256)], cot_send, cot_recv, partner)

    def y_remote(d):
        return remote(
            dec.at[pl.ds(pl.multiple_of(((y + d) % NY) * PIECE, 8), PIECE)],
            ry.at[d - 1],
            y_send.at[d - 1],
            y_recv.at[d - 1],
            y_peer(d),
        )

    mine = pl.ds(pl.multiple_of(y * PIECE, 8), PIECE)
    x_remote = remote(rx.at[0], rx.at[1], x_send, x_recv, x_near)

    def g_remote(d):
        return remote(avg.at[mine], avg.at[mine], g_send.at[d - 1], g_recv.at[d - 1], y_peer(d))

    def b_remote(i):
        rows = pl.ds(3 * span_at(i), 3)
        return remote(B.at[rows], XB.at[rows], b_send.at[i], b_recv.at[i], x_far(c))

    def dest_at(way, s):
        return (z + HOPS - s) % NZ if way == 0 else (z + NZ - HOPS + s) % NZ

    def ring_remote(P_, way, k, s):
        buf, ring, send, recv = P_
        return remote(
            buf.at[dest_at(way, s) * 2 + k],
            ring.at[way, k, s],
            send.at[way, k, s],
            recv.at[way, k, s],
            z_next if way == 0 else z_prev,
        )

    part_a = (A, ring_a, ra_send, ra_recv)
    part_b = (B, ring_b, rb_send, rb_recv)
    order = ((0, 0), (1, 1), (1, 0), (0, 1))

    def ring_step(P_, way, k, s):
        buf, ring = P_[:2]
        ring_remote(P_, way, k, s - 1).wait_recv()
        at = dest_at(way, s) * 2 + k
        buf[at] = (buf[at].astype(f32) + ring[way, k, s - 1].astype(f32)).astype(buf.dtype)
        ring_remote(P_, way, k, s).start()
        ring_remote(P_, way, k, s - 1).wait_send()

    def ring_0(P_):
        ring_remote(P_, 0, 0, 0).start()
        ring_remote(P_, 1, 1, 0).start()

    def ring_1(P_):
        ring_remote(P_, 0, 1, 1).start()
        ring_remote(P_, 1, 0, 1).start()
        ring_step(P_, 0, 0, 1)
        ring_step(P_, 1, 1, 1)

    def ring_s(P_, s):
        for way, k in order:
            ring_step(P_, way, k, s)

    lanes = lax.broadcasted_iota(jnp.int32, (128, LANES), 1)

    def do_spans(lo, hi):
        @pl.loop(lo, hi)
        def _(i):
            t = span_at(i)
            tok_remote(i).wait_recv()
            for q in range(4):
                X = tok2[:, pl.ds(pl.multiple_of(t * SPAN + 128 * q, 128), 128)]
                out = lax.dot_general(X, cot[...], (((0,), (0,)), ((), ())), preferred_element_type=f32)
                for j in range(2):
                    S[j, 128 * q : 128 * q + 128, :] = out[:, 128 * j : 128 * j + 128]
                S[2, 128 * q : 128 * q + 128, 0:32] = out[:, 256:288]
            flatten_span(S, flat, lanes)
            for j in range(3):
                A[3 * t + j] = flat[SHARD * j : SHARD * j + LATE, :].astype(A.dtype)
                B[3 * t + j] = flat[SHARD * j + LATE : SHARD * (j + 1), :].astype(B.dtype)

            @pl.when(other)
            def _():
                b_remote(i).start()

    def add_spans(lo, hi):
        @pl.loop(lo, hi)
        def _(i):
            t = span_at(i)
            b_remote(i).wait_recv()
            for j in range(3):
                B[3 * t + j] = (B[3 * t + j].astype(f32) + XB[3 * t + j].astype(f32)).astype(B.dtype)

    pl.semaphore_wait(barrier, 6 + n_near)
    cot_remote.start()

    @pl.loop(0, SPANS)
    def _(i):
        tok_remote(i).start()

    pass_on(0)
    S[2] = jnp.zeros((SPAN, LANES), f32)
    tok_copy.wait()
    cot_copy.wait()
    cot_remote.wait_recv()
    cot[...] = cot2[...].astype(f32).T.astype(cot.dtype)

    do_spans(0, 2)
    ring_0(part_a)

    w_copy.wait()
    s_copy.wait()
    delta = sv[...] - wv[...]
    scale = (jnp.max(jnp.abs(delta), axis=1, keepdims=True) / code_limit + scale_eps).astype(jnp.bfloat16)
    scale = scale.astype(f32)
    dec[...] = (delta / scale).astype(jnp.bfloat16).astype(f32) * scale

    do_spans(2, 3)
    ring_1(part_a)
    heard(0)
    pass_on(1)
    do_spans(3, 6)

    @pl.when(own)
    def _():
        add_spans(0, 2)
        ring_0(part_b)

    ring_s(part_a, 2)
    heard(1)
    pass_on(2)
    do_spans(6, 8)

    @pl.when(own)
    def _():
        add_spans(2, 3)
        ring_1(part_b)

    ring_s(part_a, 3)
    heard(2)

    @pl.loop(1, NY)
    def _(d):
        y_remote(d).start()

    @pl.when(own)
    def _():
        add_spans(3, 4)
        ring_s(part_b, 2)

    ring_s(part_a, 4)

    @pl.loop(0, SPANS)
    def _(i):
        tok_remote(i).wait_send()

    cot_remote.wait_send()

    @pl.when(own)
    def _():
        add_spans(4, 6)
        ring_s(part_b, 3)

    ring_s(part_a, 5)

    @pl.loop(1, NY)
    def _(d):
        y_remote(d).wait()

    total = dec[mine, :]
    for d in range(NY - 1):
        total = total + ry[d]
    rx[0] = total
    x_remote.start()

    @pl.when(own)
    def _():
        add_spans(6, 7)
        ring_s(part_b, 4)

    def spread():
        x_remote.wait()
        avg[mine, :] = (rx[0] + rx[1]) / (2 * NY)

        @pl.loop(1, NY)
        def _(d):
            g_remote(d).start()

    @pl.when(own)
    def _():
        spread()
        add_spans(7, 8)
        ring_s(part_b, 5)

    def fin(P_, k, slot, dst, device):
        return remote((Fa if P_ is part_a else Fb).at[k], dst, fin_send.at[slot], fin_recv.at[slot], device)

    def a_partner(k):
        return fin(part_a, k, 0, xa.at[0], partner)

    def a_far(k):
        return remote(Fa.at[k], xa.at[1], fin_send.at[1 + k], fin_recv.at[1], x_far(k))

    def b_partner(k):
        return fin(part_b, k, 3, xb, partner)

    def finish(P_, k):
        buf, ring = P_[:2]
        ring_remote(P_, 0, k, HOPS - 1).wait_recv()
        ring_remote(P_, 1, k, HOPS - 1).wait_recv()
        return buf[z * 2 + k].astype(f32) + ring[0, k, HOPS - 1].astype(f32) + ring[1, k, HOPS - 1].astype(f32)

    near_first = jnp.where(own, 1 - c, 0)
    for k in (near_first, 1 - near_first):
        Fa[k] = finish(part_a, k).astype(Fa.dtype)

        @pl.when(other)
        def _():
            a_far(k).start()

        @pl.when(own & (c != k))
        def _():
            a_partner(k).start()

    @pl.when(other)
    def _():
        spread()

    @pl.when(own)
    def _():
        Fb[1 - c] = finish(part_b, 1 - c).astype(Fb.dtype)
        b_partner(1 - c).start()
        grad[LATE:, :] = finish(part_b, c)

    a_far(0).wait_recv()

    @pl.when(own)
    def _():
        grad[:LATE, :] = Fa[c].astype(f32) + xa[1].astype(f32)

    @pl.when(other)
    def _():
        a_partner(0).wait_recv()
        grad[:LATE, :] = xa[0].astype(f32) + xa[1].astype(f32)
        b_partner(0).wait_recv()
        grad[LATE:, :] = xb[...].astype(f32)

    grad_copy = pltpu.make_async_copy(grad, grad_hbm, local_sem.at[5])
    grad_copy.start()

    @pl.loop(1, NY)
    def _(d):
        g_remote(d).wait()

    avg_copy = pltpu.make_async_copy(avg, avg_hbm, local_sem.at[4])
    avg_copy.start()

    def ring_sent(P_):
        for way, k in order:
            ring_remote(P_, way, k, HOPS - 1).wait_send()

    ring_sent(part_a)

    @pl.when(own)
    def _():
        a_partner(0).wait_send()
        b_partner(0).wait_send()
        ring_sent(part_b)

    @pl.when(other)
    def _():
        a_far(0).wait_send()
        a_far(1).wait_send()

        @pl.loop(0, SPANS)
        def _(i):
            b_remote(i).wait_send()

    avg_copy.wait()
    grad_copy.wait()


def body(tokens, cotangent, weights, start_weights, momentum):
    shape = (SHARD, LANES)
    ny = lax.axis_size("rep") // 2
    piece = SHARD // ny
    f32, bf16 = jnp.float32, jnp.bfloat16
    dma = pltpu.SemaphoreType.DMA
    out = jax.ShapeDtypeStruct(shape, f32)
    late, early = (LATE, LANES), (EARLY, LANES)
    shards = 2 * NZ
    grad, average = pl.pallas_call(
        kernel,
        out_shape=(out, out),
        in_specs=[pl.BlockSpec(memory_space=pltpu.HBM)] * 4,
        out_specs=[pl.BlockSpec(memory_space=pltpu.HBM)] * 2,
        scratch_shapes=[
            pltpu.VMEM((512, SPAN * SPANS), bf16),
            pltpu.VMEM((288, 512), bf16),
            pltpu.VMEM((512, 288), bf16),
            pltpu.VMEM(shape, f32),
            pltpu.VMEM(shape, f32),
            pltpu.VMEM(shape, f32),
            pltpu.VMEM(shape, f32),
            pltpu.VMEM((ny - 1, piece, LANES), f32),
            pltpu.VMEM((2, piece, LANES), f32),
            pltpu.VMEM((3, SPAN, LANES), f32),
            pltpu.VMEM((1152, LANES), f32),
            pltpu.VMEM((shards, *late), bf16),
            pltpu.VMEM((shards, *early), bf16),
            pltpu.VMEM((shards, *early), bf16),
            pltpu.VMEM((2, 2, HOPS, *late), bf16),
            pltpu.VMEM((2, 2, HOPS, *early), bf16),
            pltpu.VMEM((2, *late), bf16),
            pltpu.VMEM((2, *early), bf16),
            pltpu.VMEM((2, *late), bf16),
            pltpu.VMEM(early, bf16),
            pltpu.VMEM(shape, f32),
            dma((6,)),
            dma((SPANS,)),
            dma((SPANS,)),
            dma,
            dma,
            dma((ny - 1,)),
            dma((ny - 1,)),
            dma,
            dma,
            pltpu.SemaphoreType.REGULAR((len(STEPS), max(ny // 2 - 1, 1))),
            dma((ny - 1,)),
            dma((ny - 1,)),
            dma((SPANS,)),
            dma((SPANS,)),
            dma((2, 2, HOPS)),
            dma((2, 2, HOPS)),
            dma((2, 2, HOPS)),
            dma((2, 2, HOPS)),
            dma((4,)),
            dma((4,)),
        ],
        compiler_params=pltpu.CompilerParams(
            collective_id=0, has_side_effects=True, vmem_limit_bytes=60 << 20
        ),
    )(tokens[0], cotangent[0].T, weights.reshape(shape), start_weights.reshape(shape))
    grad, average = grad.reshape(-1), average.reshape(-1)
    new_momentum = nesterov_mu * momentum + average
    new_start = start_weights - outer_rate * (nesterov_mu * new_momentum + average)
    current = weights[0] - inner_rate * grad
    mixed_weights = mix_weight * current + (1.0 - mix_weight) * new_start
    return mixed_weights[None], new_momentum, new_start


def solution(mesh):
    placed = (
        P("rep", "fsdp", None),
        P("rep", "fsdp", None),
        P("rep", "fsdp"),
        P("fsdp"),
        P("fsdp"),
    )
    return jax.shard_map(
        body,
        mesh=mesh,
        in_specs=placed,
        out_specs=(P("rep", "fsdp"), P("fsdp"), P("fsdp")),
        check_vma=False,
    )
```

```python
import jax
import jax.numpy as jnp
from jax import lax
from jax.experimental import pallas as pl
from jax.experimental.pallas import tpu as pltpu
from jax.sharding import PartitionSpec as P

code_limit = 448.0
scale_eps = 1e-06
inner_rate = 0.5
outer_rate = 0.7
nesterov_mu = 0.9
mix_weight = 0.5

MESH = pl.DeviceIdType.MESH
NZ = 12
LANES = 128
SHARD = 384
LATE = 192
EARLY = SHARD - LATE
STEPS = (-2, -1, 1, 2)
SPAN = 512
SPANS = 8
HOPS = NZ // 2


def flatten_span(S, flat, lanes):
    A = [[S[j, pl.ds(k, 128, stride=4), :] for j in range(3)] for k in range(4)]
    R = [A[0]] + [[pltpu.roll(A[k][j], 32 * k, 1) for j in range(3)] for k in (1, 2, 3)]
    m32, m64, m96 = lanes < 32, lanes < 64, lanes < 96
    tiles = [
        R[0][0],
        R[0][1],
        jnp.where(m32, R[0][2], R[1][0]),
        jnp.where(m32, R[1][0], R[1][1]),
        jnp.where(m32, R[1][1], jnp.where(m64, R[1][2], R[2][0])),
        jnp.where(m64, R[2][0], R[2][1]),
        jnp.where(m64, R[2][1], jnp.where(m96, R[2][2], R[3][0])),
        jnp.where(m96, R[3][0], R[3][1]),
        jnp.where(m96, R[3][1], R[3][2]),
    ]
    for j in range(9):
        flat[pl.ds(j, 128, stride=9), :] = tiles[j]


def kernel(
    tok_hbm, cot_hbm, w_hbm, s_hbm,
    grad_hbm, avg_hbm,
    tok2, cot2, cot, wv, sv, dec, avg, ry, rx, S, flat, A, B, XB, ring_a, ring_b, Fa, Fb, xa, xb, grad,
    local_sem, tok_send, tok_recv, cot_send, cot_recv, y_send, y_recv, x_send, x_recv,
    near_sem, g_send, g_recv, b_send, b_recv, ra_send, ra_recv, rb_send, rb_recv, fin_send, fin_recv,
):
    f32 = jnp.float32
    NY = ry.shape[0] + 1
    PIECE = SHARD // NY
    rounds = NY // 2 - 1
    rep = lax.axis_index("rep")
    pos = lax.axis_index("fsdp")
    xl, y = rep // NY, rep % NY
    a, z, c = pos // (2 * NZ), (pos % (2 * NZ)) // 2, pos % 2
    own = c == a
    other = jnp.logical_not(own)

    partner = (rep, pos + 1 - 2 * c)
    z_next = (rep, a * 2 * NZ + ((z + 1) % NZ) * 2 + c)
    z_prev = (rep, a * 2 * NZ + ((z + NZ - 1) % NZ) * 2 + c)
    x_near = ((1 - xl) * NY + y, pos)

    def x_far(core):
        return (rep, (1 - a) * 2 * NZ + z * 2 + core)

    def y_peer(d):
        return (xl * NY + (y + d) % NY, pos)

    def remote(src, dst, send, recv, device):
        return pltpu.make_async_remote_copy(
            src_ref=src, dst_ref=dst, send_sem=send, recv_sem=recv, device_id=device, device_id_type=MESH
        )

    turn = NY // 2
    place = jnp.where(y < turn, y, NY + turn - 1 - y)

    def y_near(o):
        at = place + o
        return (xl * NY + jnp.where(at < turn, at, NY + turn - 1 - at), pos)

    def each_near(act):
        for j, o in enumerate(STEPS):

            @pl.when((place + o >= 0) & (place + o < NY))
            def _():
                act(j, o)

    barrier = pltpu.get_barrier_semaphore()
    for dev in (partner, z_next, z_prev, x_near, x_far(0), x_far(1)):
        pl.semaphore_signal(barrier, inc=1, device_id=dev, device_id_type=MESH)
    each_near(lambda j, o: pl.semaphore_signal(barrier, inc=1, device_id=y_near(o), device_id_type=MESH))
    n_near = jnp.minimum(place, 2) + jnp.minimum(NY - 1 - place, 2)

    w_copy = pltpu.make_async_copy(w_hbm, wv, local_sem.at[0])
    s_copy = pltpu.make_async_copy(s_hbm, sv, local_sem.at[1])
    cot_copy = pltpu.make_async_copy(cot_hbm, cot2.at[:, pl.ds(0, 256)], local_sem.at[2])
    half = SPAN * SPANS
    tok_copy = pltpu.make_async_copy(
        tok_hbm.at[:, pl.ds(pl.multiple_of(c * half, half), half)], tok2.at[pl.ds(0, 256)], local_sem.at[3]
    )
    cot_copy.start()
    tok_copy.start()
    w_copy.start()
    s_copy.start()

    def pass_on(r):
        if r < rounds:
            each_near(
                lambda j, o: pl.semaphore_signal(
                    near_sem.at[3 - j, r], inc=1, device_id=y_near(o), device_id_type=MESH
                )
            )

    def heard(r):
        if r < rounds:
            each_near(lambda j, o: pl.semaphore_wait(near_sem.at[j, r], 1))

    far = (z + HOPS) % NZ

    def pick(table, i):
        return sum(jnp.where(i == j, v, 0) for j, v in enumerate(table))

    def span_at(i):
        outer = pick((0, 1, -1, -2, 2, -3, 3, 4), i)
        inner = pick((0, 1, 2, -1, 3, -2, 4, -3), i)
        third = far % 3
        o = jnp.where(third == 1, inner, jnp.where(third == 0, outer, 1 - outer))
        return (2 * (far // 3) + o + 2 * SPANS) % SPANS

    def tok_remote(i):
        t = span_at(i)
        return remote(
            tok_hbm.at[:, pl.ds(pl.multiple_of((1 - c) * half + t * SPAN, SPAN), SPAN)],
            tok2.at[pl.ds(256, 256), pl.ds(pl.multiple_of(t * SPAN, SPAN), SPAN)],
            tok_send.at[i],
            tok_recv.at[i],
            partner,
        )

    cot_remote = remote(cot_hbm, cot2.at[:, pl.ds(256, 256)], cot_send, cot_recv, partner)

    def y_remote(d):
        return remote(
            dec.at[pl.ds(pl.multiple_of(((y + d) % NY) * PIECE, 8), PIECE)],
            ry.at[d - 1],
            y_send.at[d - 1],
            y_recv.at[d - 1],
            y_peer(d),
        )

    mine = pl.ds(pl.multiple_of(y * PIECE, 8), PIECE)
    x_remote = remote(rx.at[0], rx.at[1], x_send, x_recv, x_near)

    def g_remote(d):
        return remote(avg.at[mine], avg.at[mine], g_send.at[d - 1], g_recv.at[d - 1], y_peer(d))

    def b_remote(i):
        rows = pl.ds(3 * span_at(i), 3)
        return remote(B.at[rows], XB.at[rows], b_send.at[i], b_recv.at[i], x_far(c))

    def dest_at(way, s):
        return (z + HOPS - s) % NZ if way == 0 else (z + NZ - HOPS + s) % NZ

    def ring_remote(P_, way, k, s):
        buf, ring, send, recv = P_
        return remote(
            buf.at[dest_at(way, s) * 2 + k],
            ring.at[way, k, s],
            send.at[way, k, s],
            recv.at[way, k, s],
            z_next if way == 0 else z_prev,
        )

    part_a = (A, ring_a, ra_send, ra_recv)
    part_b = (B, ring_b, rb_send, rb_recv)
    order = ((0, 0), (1, 1), (1, 0), (0, 1))

    def ring_step(P_, way, k, s):
        buf, ring = P_[:2]
        ring_remote(P_, way, k, s - 1).wait_recv()
        at = dest_at(way, s) * 2 + k
        buf[at] = (buf[at].astype(f32) + ring[way, k, s - 1].astype(f32)).astype(buf.dtype)
        ring_remote(P_, way, k, s).start()
        ring_remote(P_, way, k, s - 1).wait_send()

    def ring_0(P_):
        ring_remote(P_, 0, 0, 0).start()
        ring_remote(P_, 1, 1, 0).start()

    def ring_1(P_):
        ring_remote(P_, 0, 1, 1).start()
        ring_remote(P_, 1, 0, 1).start()
        ring_step(P_, 0, 0, 1)
        ring_step(P_, 1, 1, 1)

    def ring_s(P_, s):
        for way, k in order:
            ring_step(P_, way, k, s)

    lanes = lax.broadcasted_iota(jnp.int32, (128, LANES), 1)

    def do_spans(lo, hi):
        @pl.loop(lo, hi)
        def _(i):
            t = span_at(i)
            tok_remote(i).wait_recv()
            for q in range(4):
                X = tok2[:, pl.ds(pl.multiple_of(t * SPAN + 128 * q, 128), 128)]
                out = lax.dot_general(X, cot[...], (((0,), (0,)), ((), ())), preferred_element_type=f32)
                for j in range(2):
                    S[j, 128 * q : 128 * q + 128, :] = out[:, 128 * j : 128 * j + 128]
                S[2, 128 * q : 128 * q + 128, 0:32] = out[:, 256:288]
            flatten_span(S, flat, lanes)
            for j in range(3):
                A[3 * t + j] = flat[SHARD * j : SHARD * j + LATE, :].astype(A.dtype)
                B[3 * t + j] = flat[SHARD * j + LATE : SHARD * (j + 1), :].astype(B.dtype)

            @pl.when(other)
            def _():
                b_remote(i).start()

    def add_spans(lo, hi):
        @pl.loop(lo, hi)
        def _(i):
            t = span_at(i)
            b_remote(i).wait_recv()
            for j in range(3):
                B[3 * t + j] = (B[3 * t + j].astype(f32) + XB[3 * t + j].astype(f32)).astype(B.dtype)

    pl.semaphore_wait(barrier, 6 + n_near)
    cot_remote.start()

    @pl.loop(0, SPANS)
    def _(i):
        tok_remote(i).start()

    pass_on(0)

    w_copy.wait()
    s_copy.wait()
    delta = sv[...] - wv[...]
    scale = (jnp.max(jnp.abs(delta), axis=1, keepdims=True) / code_limit + scale_eps).astype(jnp.bfloat16)
    scale = scale.astype(f32)
    dec[...] = (delta / scale).astype(jnp.bfloat16).astype(f32) * scale

    S[2] = jnp.zeros((SPAN, LANES), f32)
    tok_copy.wait()
    cot_copy.wait()
    cot_remote.wait_recv()
    cot[...] = cot2[...].astype(f32).T.astype(cot.dtype)

    do_spans(0, 2)
    ring_0(part_a)

    do_spans(2, 3)
    ring_1(part_a)
    heard(0)
    pass_on(1)
    do_spans(3, 6)

    @pl.when(own)
    def _():
        add_spans(0, 2)
        ring_0(part_b)

    ring_s(part_a, 2)
    heard(1)
    pass_on(2)
    do_spans(6, 8)

    @pl.when(own)
    def _():
        add_spans(2, 3)
        ring_1(part_b)

    ring_s(part_a, 3)
    heard(2)

    @pl.loop(1, NY)
    def _(d):
        y_remote(d).start()

    @pl.when(own)
    def _():
        add_spans(3, 4)
        ring_s(part_b, 2)

    ring_s(part_a, 4)

    @pl.loop(0, SPANS)
    def _(i):
        tok_remote(i).wait_send()

    cot_remote.wait_send()

    @pl.when(own)
    def _():
        add_spans(4, 6)
        ring_s(part_b, 3)

    ring_s(part_a, 5)

    @pl.loop(1, NY)
    def _(d):
        y_remote(d).wait()

    total = dec[mine, :]
    for d in range(NY - 1):
        total = total + ry[d]
    rx[0] = total
    x_remote.start()

    @pl.when(own)
    def _():
        add_spans(6, 7)
        ring_s(part_b, 4)

    def spread():
        x_remote.wait()
        avg[mine, :] = (rx[0] + rx[1]) / (2 * NY)

        @pl.loop(1, NY)
        def _(d):
            g_remote(d).start()

    @pl.when(own)
    def _():
        spread()
        add_spans(7, 8)
        ring_s(part_b, 5)

    def fin(P_, k, slot, dst, device):
        return remote((Fa if P_ is part_a else Fb).at[k], dst, fin_send.at[slot], fin_recv.at[slot], device)

    def a_partner(k):
        return fin(part_a, k, 0, xa.at[0], partner)

    def a_far(k):
        return remote(Fa.at[k], xa.at[1], fin_send.at[1 + k], fin_recv.at[1], x_far(k))

    def b_partner(k):
        return fin(part_b, k, 3, xb, partner)

    def finish(P_, k):
        buf, ring = P_[:2]
        ring_remote(P_, 0, k, HOPS - 1).wait_recv()
        ring_remote(P_, 1, k, HOPS - 1).wait_recv()
        return buf[z * 2 + k].astype(f32) + ring[0, k, HOPS - 1].astype(f32) + ring[1, k, HOPS - 1].astype(f32)

    near_first = jnp.where(own, 1 - c, 0)
    for k in (near_first, 1 - near_first):
        Fa[k] = finish(part_a, k).astype(Fa.dtype)

        @pl.when(other)
        def _():
            a_far(k).start()

        @pl.when(own & (c != k))
        def _():
            a_partner(k).start()

    @pl.when(other)
    def _():
        spread()

    @pl.when(own)
    def _():
        Fb[1 - c] = finish(part_b, 1 - c).astype(Fb.dtype)
        b_partner(1 - c).start()
        grad[LATE:, :] = finish(part_b, c)

    a_far(0).wait_recv()

    @pl.when(own)
    def _():
        grad[:LATE, :] = Fa[c].astype(f32) + xa[1].astype(f32)

    @pl.when(other)
    def _():
        a_partner(0).wait_recv()
        grad[:LATE, :] = xa[0].astype(f32) + xa[1].astype(f32)
        b_partner(0).wait_recv()
        grad[LATE:, :] = xb[...].astype(f32)

    grad_copy = pltpu.make_async_copy(grad, grad_hbm, local_sem.at[5])
    grad_copy.start()

    @pl.loop(1, NY)
    def _(d):
        g_remote(d).wait()

    avg_copy = pltpu.make_async_copy(avg, avg_hbm, local_sem.at[4])
    avg_copy.start()

    def ring_sent(P_):
        for way, k in order:
            ring_remote(P_, way, k, HOPS - 1).wait_send()

    ring_sent(part_a)

    @pl.when(own)
    def _():
        a_partner(0).wait_send()
        b_partner(0).wait_send()
        ring_sent(part_b)

    @pl.when(other)
    def _():
        a_far(0).wait_send()
        a_far(1).wait_send()

        @pl.loop(0, SPANS)
        def _(i):
            b_remote(i).wait_send()

    avg_copy.wait()
    grad_copy.wait()


def body(tokens, cotangent, weights, start_weights, momentum):
    shape = (SHARD, LANES)
    ny = lax.axis_size("rep") // 2
    piece = SHARD // ny
    f32, bf16 = jnp.float32, jnp.bfloat16
    dma = pltpu.SemaphoreType.DMA
    out = jax.ShapeDtypeStruct(shape, f32)
    late, early = (LATE, LANES), (EARLY, LANES)
    shards = 2 * NZ
    grad, average = pl.pallas_call(
        kernel,
        out_shape=(out, out),
        in_specs=[pl.BlockSpec(memory_space=pltpu.HBM)] * 4,
        out_specs=[pl.BlockSpec(memory_space=pltpu.HBM)] * 2,
        scratch_shapes=[
            pltpu.VMEM((512, SPAN * SPANS), bf16),
            pltpu.VMEM((288, 512), bf16),
            pltpu.VMEM((512, 288), bf16),
            pltpu.VMEM(shape, f32),
            pltpu.VMEM(shape, f32),
            pltpu.VMEM(shape, f32),
            pltpu.VMEM(shape, f32),
            pltpu.VMEM((ny - 1, piece, LANES), f32),
            pltpu.VMEM((2, piece, LANES), f32),
            pltpu.VMEM((3, SPAN, LANES), f32),
            pltpu.VMEM((1152, LANES), f32),
            pltpu.VMEM((shards, *late), bf16),
            pltpu.VMEM((shards, *early), bf16),
            pltpu.VMEM((shards, *early), bf16),
            pltpu.VMEM((2, 2, HOPS, *late), bf16),
            pltpu.VMEM((2, 2, HOPS, *early), bf16),
            pltpu.VMEM((2, *late), bf16),
            pltpu.VMEM((2, *early), bf16),
            pltpu.VMEM((2, *late), bf16),
            pltpu.VMEM(early, bf16),
            pltpu.VMEM(shape, f32),
            dma((6,)),
            dma((SPANS,)),
            dma((SPANS,)),
            dma,
            dma,
            dma((ny - 1,)),
            dma((ny - 1,)),
            dma,
            dma,
            pltpu.SemaphoreType.REGULAR((len(STEPS), max(ny // 2 - 1, 1))),
            dma((ny - 1,)),
            dma((ny - 1,)),
            dma((SPANS,)),
            dma((SPANS,)),
            dma((2, 2, HOPS)),
            dma((2, 2, HOPS)),
            dma((2, 2, HOPS)),
            dma((2, 2, HOPS)),
            dma((4,)),
            dma((4,)),
        ],
        compiler_params=pltpu.CompilerParams(
            collective_id=0, has_side_effects=True, vmem_limit_bytes=60 << 20
        ),
    )(tokens[0], cotangent[0].T, weights.reshape(shape), start_weights.reshape(shape))
    grad, average = grad.reshape(-1), average.reshape(-1)
    new_momentum = nesterov_mu * momentum + average
    new_start = start_weights - outer_rate * (nesterov_mu * new_momentum + average)
    current = weights[0] - inner_rate * grad
    mixed_weights = mix_weight * current + (1.0 - mix_weight) * new_start
    return mixed_weights[None], new_momentum, new_start


def solution(mesh):
    placed = (
        P("rep", "fsdp", None),
        P("rep", "fsdp", None),
        P("rep", "fsdp"),
        P("fsdp"),
        P("fsdp"),
    )
    return jax.shard_map(
        body,
        mesh=mesh,
        in_specs=placed,
        out_specs=(P("rep", "fsdp"), P("fsdp"), P("fsdp")),
        check_vma=False,
    )
```
